256 devices in a mesh: seq: 16 (over x, z_hi, core), tensor: 16 (over y, z_lo).
Axes of the slice: x: 4, y: 4, z: 8 (z_hi: 2, z_lo: 4; z = z_hi * 4 + z_lo), core: 2. Of those that a mesh axis runs over, the one named last changes fastest.
Arguments:
- queries: bfloat16 [32, 1024, 4096], P('tensor', None, 'seq'), may hold values from -6 to 6
- keys: bfloat16 [32, 1024, 4096], P('tensor', None, 'seq'), may hold values from -6 to 6
- values: bfloat16 [32, 1024, 4096], P('tensor', None, 'seq'), may hold values from -6 to 6
- ffn_hidden: bfloat16 [32, 1024, 11264], P(None, 'seq', 'tensor'), may hold values from -6 to 6
- out_grad: bfloat16 [32, 1024, 4096], P('tensor', 'seq'), may hold values from -6 to 6
- butterfly: int32 [64, 16], P('tensor'), may hold values from 0 to 63, as said below
- segments: int32 [32, 1024], P('tensor'), may hold values from 0 to 3, never falling along the last dimension, each value on 1 to 512 neighbouring positions
- up_weight: bfloat16 [64, 16, 64, 176], P('tensor'), may hold values from -0.1875 to 0.1875
- down_weight: bfloat16 [64, 16, 64, 176], P('tensor'), may hold values from -0.1875 to 0.1875
Outputs:
- query_grad: bfloat16 [32, 1024, 4096], P('tensor', None, 'seq')
- key_grad: bfloat16 [32, 1024, 4096], P('tensor', None, 'seq')
- value_grad: bfloat16 [32, 1024, 4096], P('tensor', None, 'seq')
The draws below stay inside these ranges and needn't reach their ends.
Inputs may be any that keep to these rules, and one draw needn't show every extreme that they name: `butterfly`: row c lists 16 distinct model-width blocks: c XOR a combination of 4 of the 6 index bits, the same 4 bits for every row; each block is named in exactly 16 rows.
All inputs are finite; a program needn't handle non-finite values.
Results may differ from the reference program's by a relative error of at most 0.03.
Values may be sent and summed in bfloat16 or wider, within the bound.
No kernel may reach another device: no remote copies, remote signals or barrier semaphores. Data moves between devices by JAX's collectives and lax.ppermute only.
A program may use at most 256 MiB of HBM per device.

```python
import math
import jax
import jax.numpy as jnp
import numpy as np
from jax import lax

D = 4096
HEADS = 32
HD = 128
FF = 11264
NBLK = 64
NNZ = 16
DB = 64
FB = 176
LEN = 1024
SEQS = 32
N_TENSOR = 16


def draw_queries(key, part):
    key = jax.random.fold_in(key, 11)
    drawn = jnp.clip(jax.random.normal(key, (SEQS, LEN, D), jnp.float32), -6.0, 6.0)
    return drawn.astype(jnp.bfloat16)


def draw_keys(key, part):
    key = jax.random.fold_in(key, 23)
    drawn = jnp.clip(jax.random.normal(key, (SEQS, LEN, D), jnp.float32), -6.0, 6.0)
    return drawn.astype(jnp.bfloat16)


def draw_butterfly(key, part):
    key = jax.random.fold_in(key, 5)
    bit_order = jax.random.permutation(key, 6)[:4].astype(jnp.int32)
    slot_ids = jnp.arange(NNZ, dtype=jnp.int32)
    bit_spread = jnp.zeros((NNZ,), jnp.int32)
    for bit_index in range(4):
        picked = jnp.bitwise_and(jnp.right_shift(slot_ids, bit_index), 1)
        bit_spread = bit_spread + jnp.left_shift(picked, bit_order[bit_index])
    block_rows = jnp.bitwise_xor(jnp.arange(NBLK, dtype=jnp.int32)[:, None], bit_spread[None, :])
    return block_rows.astype(jnp.int32)


def steps_of(stream_key, shape, cuts, low, high):
    def one(position, parts):
        steps = jax.random.uniform(jax.random.fold_in(jax.random.fold_in(stream_key, 6), position), (parts,), jnp.float32, low / len(cuts), high / len(cuts))
        return jnp.repeat(jnp.exp(steps), shape[position] // parts).reshape((-1,) + (1,) * (len(shape) - position - 1))

    gain = one(*cuts[0])
    for cut in cuts[1:]:
        gain = gain * one(*cut)
    return gain


def length_profile(count, total, bound, slope):
    portions = [(1 << 20) // math.isqrt(rank ** slope) + 1 for rank in range(2, count + 1)]
    rest, holding = total - bound - (count - 1), [1] * (count - 1)
    while rest > 0:
        candidates = [i for i in range(count - 1) if holding[i] < bound]
        whole, remaining = sum([portions[i] for i in candidates]), rest
        for i in candidates:
            addition = min(bound - holding[i], max(1, remaining * portions[i] // whole), rest)
            holding[i] = holding[i] + addition
            rest = rest - addition
    return np.array([bound] + holding)


def uneven(stream_key, count, total, limit, skew):
    if count == 2:
        one = jax.random.randint(stream_key, (), max(1, total - limit), min(limit, total - 1) + 1)
        return jnp.stack([one, total - one])
    sizes = jnp.asarray(length_profile(count, total, limit, skew), jnp.int32)
    pairs = (count - 1) // 2
    donor, sink = sizes[1:1 + 2 * pairs:2], sizes[2:2 + 2 * pairs:2]
    slack = jnp.minimum(donor - 1, limit - sink)
    moved = jax.random.randint(jax.random.fold_in(stream_key, 1), (pairs,), 0, 1 << 20) % (slack + 1)
    sizes = sizes.at[1:1 + 2 * pairs:2].set(donor - moved).at[2:2 + 2 * pairs:2].set(sink + moved)
    return sizes[jax.random.permutation(jax.random.fold_in(stream_key, 2), count)]


def normal_values(key, shape, width, limit, shards=(), kind=jnp.bfloat16):
    values = width * jax.random.normal(key, shape, jnp.float32)
    if shards:
        values = values * steps_of(key, shape, shards, -0.22, 0.18)
    return jnp.clip(values, -limit, limit).astype(kind)


def setup_inputs(seed: int = 0) -> dict:
    seeds = jax.random.split(jax.random.key(seed), 10)
    return {
        "queries": draw_queries(jax.random.fold_in(seeds[9], 71), 0),
        "keys": draw_keys(jax.random.fold_in(seeds[9], 71), 0),
        "values": normal_values(seeds[2], (SEQS, LEN, D), 1.0, 6.0, ((0, 16), (2, 16))),
        "ffn_hidden": normal_values(seeds[3], (SEQS, LEN, FF), 1.0, 6.0, ((1, 16), (2, 16))),
        "out_grad": normal_values(seeds[4], (SEQS, LEN, D), 1.0, 6.0, ((0, 16), (1, 16))),
        "butterfly": draw_butterfly(jax.random.fold_in(seeds[9], 71), 0),
        "segments": jax.vmap(lambda own: jnp.searchsorted(jnp.cumsum(uneven(own, 4, LEN, LEN // 2, 2)), jnp.arange(LEN), side="right"))(jax.random.split(seeds[6], SEQS)).reshape((SEQS, LEN)).astype(jnp.int32),
        "up_weight": normal_values(seeds[7], (NBLK, NNZ, DB, FB), (NNZ * DB) ** -0.5, 0.1875, ((0, 16),)),
        "down_weight": normal_values(seeds[8], (NBLK, NNZ, DB, FB), (NNZ * DB) ** -0.5, 0.1875, ((0, 16),)),
    }


masked_fill = -1e+30

def gelu_slope(hidden):
    cumulative = 0.5 * (1.0 + jax.scipy.special.erf(hidden * 0.7071067811865476))
    return cumulative + hidden * jnp.exp(-0.5 * hidden * hidden) * 0.3989422804014327

def reference(queries, keys, values, ffn_hidden, out_grad, butterfly, segments, up_weight, down_weight):
    per_group = NBLK // N_TENSOR

    def ffn_one(operands):
        grad_seq, hidden_seq = operands
        grad_blocks = grad_seq.reshape(LEN, NBLK, DB)
        hidden_blocks = hidden_seq.reshape(LEN, NBLK, FB).astype(jnp.float32)
        summed = jnp.zeros((LEN, NBLK, DB), jnp.float32)
        for group_index in range(N_TENSOR):
            lower = group_index * per_group
            index_rows = butterfly[lower:lower + per_group]
            up_part = up_weight[lower:lower + per_group].astype(jnp.float32)
            down_part = down_weight[lower:lower + per_group].astype(jnp.float32)
            chosen_grad = jnp.take(grad_blocks, index_rows, axis=1).astype(jnp.float32)
            hidden_grad = jnp.einsum('tcmd,cmdf->tcf', chosen_grad, down_part)
            slope_grad = (hidden_grad * gelu_slope(hidden_blocks[:, lower:lower + per_group])).astype(jnp.bfloat16)
            contrib = jnp.einsum('tcf,cmdf->tcmd', slope_grad.astype(jnp.float32), up_part)
            placed = jnp.zeros((LEN, NBLK, DB), jnp.float32).at[:, index_rows.reshape(-1)].add(contrib.reshape(LEN, per_group * NNZ, DB))
            rounded = lax.optimization_barrier(placed.astype(jnp.bfloat16))
            summed = summed + rounded.astype(jnp.float32)
        return (grad_seq.astype(jnp.float32) + summed.reshape(LEN, D)).astype(jnp.bfloat16)
    grad_heads = lax.map(ffn_one, (out_grad, ffn_hidden))
    head_scale = 1.0 / math.sqrt(HD)

    def heads_major(array):
        return array.reshape(LEN, HEADS, HD).transpose(1, 0, 2)

    def back_order(array):
        return array.transpose(1, 0, 2).reshape(LEN, D)

    def attend(operands):
        query_seq, key_seq, value_seq, grad_seq, segment_seq = operands
        positions = jnp.arange(LEN, dtype=jnp.int32)
        visible = (positions[None, :] <= positions[:, None]) & (segment_seq[None, :] == segment_seq[:, None])

        def per_head(head_ops):
            query_head, key_head, value_head, grad_head = head_ops
            scores = jnp.dot(query_head, key_head.T, preferred_element_type=jnp.float32) * head_scale
            scores = jnp.where(visible, scores, masked_fill)
            row_peak = lax.optimization_barrier(jnp.max(scores, axis=1, keepdims=True))
            exponent = jnp.exp(scores - row_peak)
            attn_prob = exponent / lax.optimization_barrier(jnp.sum(exponent, axis=1, keepdims=True))
            prob_half = attn_prob.astype(jnp.bfloat16)
            value_grad = jnp.dot(prob_half.T, grad_head, preferred_element_type=jnp.float32)
            prob_grad = jnp.dot(grad_head, value_head.T, preferred_element_type=jnp.float32)
            row_delta = lax.optimization_barrier(jnp.sum(attn_prob * prob_grad, axis=1, keepdims=True))
            score_grad = (attn_prob * (prob_grad - row_delta)).astype(jnp.bfloat16)
            query_grad = head_scale * jnp.dot(score_grad, key_head, preferred_element_type=jnp.float32)
            key_grad = head_scale * jnp.dot(score_grad.T, query_head, preferred_element_type=jnp.float32)
            return (query_grad.astype(jnp.bfloat16), key_grad.astype(jnp.bfloat16), value_grad.astype(jnp.bfloat16))
        query_grad, key_grad, value_grad = lax.map(per_head, (heads_major(query_seq), heads_major(key_seq), heads_major(value_seq), heads_major(grad_seq)))
        return (back_order(query_grad), back_order(key_grad), back_order(value_grad))
    query_grad, key_grad, value_grad = lax.map(attend, (queries, keys, values, grad_heads, segments))
    return (query_grad, key_grad, value_grad)
```

```python
import functools
import math

import jax
import jax.numpy as jnp
from jax import lax
from jax.experimental import pallas as pl
from jax.experimental.pallas import tpu as pltpu
from jax.sharding import PartitionSpec as P

D = 4096
HD = 128
FF = 11264
NBLK = 64
NNZ = 16
DB = 64
FB = 176
LEN = 1024
ROWS = 128
MIB = 1 << 20

masked_fill = -1e30


def gelu_slope(hidden):
    cumulative = 0.5 * (1.0 + jax.scipy.special.erf(hidden * 0.7071067811865476))
    return cumulative + hidden * jnp.exp(-0.5 * hidden * hidden) * 0.3989422804014327


def flip(array, axis, mask):
    return lax.ppermute(array, axis, [(i, i ^ mask) for i in range(16)])


def swap_bits(tensor, case, piece):
    if case < 4:
        return tensor ^ (4 * piece)
    swap, other = (2, 3) if case == 4 else (3, 2)
    low, high = (tensor & 1), (tensor >> swap) & 1
    kept = (tensor & ~((1 << swap) | 1)) ^ (((piece >> 1) & 1) << other)
    return kept, low, high, swap


def source_of(tensor, case, piece):
    if case < 4:
        return swap_bits(tensor, case, piece)
    kept, low, high, swap = swap_bits(tensor, case, piece)
    return kept | (low << swap) | (high ^ (piece & 1))


def target_of(tensor, case, piece):
    if case < 4:
        return swap_bits(tensor, case, piece)
    kept, low, high, swap = swap_bits(tensor, case, piece)
    return kept | ((low ^ (piece & 1)) << swap) | high


def send_piece(array, case, piece):
    pairs = [(i, target_of(i, case, piece)) for i in range(16)]
    if all(a == b for a, b in pairs):
        return array
    return lax.ppermute(array, "tensor", pairs)


def tie(*arrays):
    return lax.optimization_barrier(arrays)


class Bits:
    def __init__(self, butterfly):
        row = butterfly[0]
        span = lax.reduce(row ^ row[0], jnp.int32(0), lax.bitwise_or, (0,))
        missing = 63 & ~span
        zpart = missing & 12
        one_z = (zpart == 4) | (zpart == 8)
        highest = missing & (missing - 1)
        swapped = jnp.where((missing & 16) != 0, 16, 32)
        swaps = (zpart == 0) & ((missing & 48) != 0)
        self.missing = missing
        self.high = jnp.where(one_z, zpart, jnp.where(swaps, swapped, highest))
        self.low = missing ^ self.high
        self.case = jnp.where(swaps, 3 + (swapped >> 4), zpart >> 2)

    def coset(self, block):
        return 2 * ((block & self.high) != 0).astype(jnp.int32) + ((block & self.low) != 0).astype(jnp.int32)

    def rank(self, block):
        total = jnp.zeros_like(block)
        below = jnp.int32(0)
        for i in range(6):
            kept = 1 - ((self.missing >> i) & 1)
            total = total + ((((block >> i) & 1) * kept) << below)
            below = below + kept
        return total

    def block(self, coset, rank):
        total = jnp.zeros_like(rank)
        below = jnp.int32(0)
        for i in range(6):
            gone = (self.missing >> i) & 1
            of_coset = jnp.where(self.high == (1 << i), coset >> 1, coset & 1)
            bit = jnp.where(gone == 1, of_coset, (rank >> below) & 1)
            total = total | (bit << i)
            below = below + 1 - gone
        return total


def half_tiles(load, first, second):
    left = pltpu.roll(load(first), 64 * (first & 1), 1)
    right = pltpu.roll(load(second), 64 * (1 - (second & 1)), 1)
    lane = lax.broadcasted_iota(jnp.int32, left.shape, 1)
    return jnp.where(lane < 64, left, right)


def gather_columns_kernel(count, table, grad, *outs):
    def load(block):
        start = pl.multiple_of((block >> 1) * 128, 128)
        return grad[:, pl.ds(start, 128)].astype(jnp.float32)

    for target, out in enumerate(outs):
        for slot in range(count):

            def tile(i, carry, target=target, out=out, slot=slot):
                at = (target * count + slot) * 16 + 2 * i
                value = half_tiles(load, table[at], table[at + 1])
                out[slot, :, pl.ds(pl.multiple_of(i * 128, 128), 128)] = value.astype(jnp.bfloat16)
                return carry

            lax.fori_loop(0, 8, tile, 0)


def gather_columns(grad, table, targets, count):
    smem = pl.BlockSpec(memory_space=pltpu.SMEM)
    vmem = pl.BlockSpec(memory_space=pltpu.VMEM)
    return pl.pallas_call(
        functools.partial(gather_columns_kernel, count),
        out_shape=[jax.ShapeDtypeStruct((count, ROWS, 1024), jnp.bfloat16)] * targets,
        in_specs=[smem, vmem],
        out_specs=[vmem] * targets,
        compiler_params=pltpu.CompilerParams(vmem_limit_bytes=24 * MIB),
        name="gather_columns",
    )(table, grad)


def pack_weights_kernel(order, *refs):
    out = refs[16]
    eye = (
        lax.broadcasted_iota(jnp.int32, (2 * DB, 2 * DB), 0) == lax.broadcasted_iota(jnp.int32, (2 * DB, 2 * DB), 1)
    ).astype(jnp.bfloat16)
    for kind in range(2):
        for local in range(4):
            pair = [refs[(kind * 4 + local) * 2 + rank][0, 0] for rank in range(2)]
            both = jnp.concatenate(pair, axis=0)
            turned = lax.dot_general(both, eye, (((0,), (0,)), ((), ())), preferred_element_type=jnp.float32)
            out[kind, local * FB:(local + 1) * FB] = turned.astype(jnp.bfloat16)


def pack_weights(down, up, order, first):
    def spec(local, rank):
        return pl.BlockSpec((1, 1, DB, FB), lambda i, order: (local, order[local * 2 + rank], 0, 0))

    grid = pltpu.PrefetchScalarGridSpec(
        num_scalar_prefetch=1,
        grid=(1,),
        in_specs=[spec(local, rank) for local in range(4) for rank in range(2)] * 2,
        out_specs=pl.BlockSpec((2, 4 * FB, 2 * DB), lambda i, order: (0, 0, 0)),
    )
    chosen = lax.dynamic_slice_in_dim(order, first, 2, 1).reshape(8)
    return pl.pallas_call(
        pack_weights_kernel,
        grid_spec=grid,
        out_shape=jax.ShapeDtypeStruct((2, 4 * FB, 2 * DB), jnp.bfloat16),
        name="pack_weights",
    )(chosen, *[down] * 8, *[up] * 8)


WEIGHT_PARTS = ((0, 0, 4), (2, 0, 4), (6, 0, 4), (4, 0, 2), (4, 2, 4), (1, 0, 4), (3, 0, 4), (7, 0, 4), (5, 0, 2), (5, 2, 4))


def ffn_kernel(count, table, slots, *refs):
    weights, slopes, grads = refs[:10], refs[10:14], refs[14:18]
    outs = refs[18:22]
    wbuf, sbuf, gbuf, acc, wsem, ssem, gsem = refs[22:]
    zpos, qpos = table[0], table[1]
    copies = []
    for i, (mask, first, last) in enumerate(WEIGHT_PARTS):
        columns = pl.ds(pl.multiple_of((qpos ^ mask) * 2 * DB, 2 * DB), 2 * DB)
        copies.append(pltpu.make_async_copy(weights[i], wbuf.at[first:last, :, :, columns], wsem.at[i]))
    for y in range(4):
        for z in range(4):
            source = slopes[y].at[pl.ds(pl.multiple_of((zpos ^ z) * ROWS, ROWS), ROWS)]
            copies.append(pltpu.make_async_copy(source, sbuf.at[y, z], ssem.at[y * 4 + z]))
    for z in range(4):
        copies.append(pltpu.make_async_copy(grads[z], gbuf.at[:, z], gsem.at[z]))
    for copy in copies:
        copy.start()
    for copy in copies:
        copy.wait()

    def one_slot(slot, carry):
        acc[...] = jnp.zeros_like(acc)

        def one_y(y, carry):
            @pl.when(table[2 + y * count + slot] != 0)
            def _():
                grad = gbuf[slot].reshape(4 * ROWS, 1024)
                hidden = lax.dot_general(
                    grad, wbuf[y, 0], (((1,), (1,)), ((), ())), preferred_element_type=jnp.float32
                )
                hidden = hidden * sbuf[y].reshape(4 * ROWS, 4 * FB).astype(jnp.float32)
                hidden = jnp.where(slots[y] == slot, hidden, 0.0).astype(jnp.bfloat16)
                acc[...] += jnp.dot(hidden, wbuf[y, 1], preferred_element_type=jnp.float32)

            return carry

        lax.fori_loop(0, 4, one_y, 0)
        for z in range(4):
            outs[z][slot] = acc[z * ROWS:(z + 1) * ROWS].astype(jnp.bfloat16)
        return carry

    lax.fori_loop(0, count, one_slot, 0)


def ffn(table, slots, weights, slopes, grads, count):
    hbm = pl.BlockSpec(memory_space=pl.ANY)
    vmem = pl.BlockSpec(memory_space=pltpu.VMEM)
    return pl.pallas_call(
        functools.partial(ffn_kernel, count),
        out_shape=[jax.ShapeDtypeStruct((count, ROWS, 1024), jnp.bfloat16)] * 4,
        in_specs=[pl.BlockSpec(memory_space=pltpu.SMEM), vmem] + [hbm] * 18,
        out_specs=[vmem] * 4,
        scratch_shapes=[
            pltpu.VMEM((4, 2, 4 * FB, 16 * DB), jnp.bfloat16),
            pltpu.VMEM((4, 4, ROWS, 4 * FB), jnp.bfloat16),
            pltpu.VMEM((count, 4, ROWS, 1024), jnp.bfloat16),
            pltpu.VMEM((4 * ROWS, 1024), jnp.float32),
            pltpu.SemaphoreType.DMA((10,)),
            pltpu.SemaphoreType.DMA((16,)),
            pltpu.SemaphoreType.DMA((4,)),
        ],
        compiler_params=pltpu.CompilerParams(vmem_limit_bytes=52 * MIB),
        cost_estimate=pl.CostEstimate(flops=6 * 10**9, bytes_accessed=24 * MIB, transcendentals=0),
        name="ffn",
    )(table, slots, *weights, *slopes, *grads)


def combine_kernel(case, table, grad, p0, p1, p2, p3, out, whole):
    parts = (p0, p1, p2, p3)
    zpos = table[64]
    if case == 3:
        for d in range(4):
            whole[zpos ^ d] = parts[d][0].astype(jnp.float32)
    elif case == 0:
        for slot in range(4):
            pair = [parts[d][slot].astype(jnp.float32) for d in range(4)]
            whole[slot] = (pair[0] + pair[1]) + (pair[2] + pair[3])
    else:
        shift = 1 if case == 2 else 0
        side = (zpos >> shift) & 1
        for value in range(2):
            chosen = [d for d in range(4) if (d >> shift) & 1 == value]
            for slot in range(2):
                whole[2 * (side ^ value) + slot] = parts[chosen[0]][slot].astype(jnp.float32) + parts[chosen[1]][
                    slot
                ].astype(jnp.float32)

    def load(position):
        start = pl.multiple_of(((position & 15) >> 1) * 128, 128)
        return whole[position >> 4, :, pl.ds(start, 128)]

    def dest(k, carry):
        for half in range(2):
            tile = 2 * k + half
            value = half_tiles(load, table[2 * tile], table[2 * tile + 1])
            own = grad[:, pl.ds(pl.multiple_of(tile * 128, 128), 128)].astype(jnp.float32)
            out[k, :, half * 128:(half + 1) * 128] = (own + value).astype(jnp.bfloat16)
        return carry

    lax.fori_loop(0, 16, dest, 0)


def combine(case, table, grad, parts):
    vmem = pl.BlockSpec(memory_space=pltpu.VMEM)
    return pl.pallas_call(
        functools.partial(combine_kernel, case),
        out_shape=jax.ShapeDtypeStruct((16, ROWS, 256), jnp.bfloat16),
        in_specs=[pl.BlockSpec(memory_space=pltpu.SMEM)] + [vmem] * 5,
        out_specs=vmem,
        scratch_shapes=[pltpu.VMEM((4, ROWS, 1024), jnp.float32)],
        compiler_params=pltpu.CompilerParams(vmem_limit_bytes=32 * MIB),
        name="combine",
    )(table, grad, *parts)


def attend_kernel(query, key, value, grad, seg_col, seg_row, dquery, dkey, dvalue, kacc, vacc):
    scale = 1.0 / math.sqrt(HD)
    step = 256
    across = (((1,), (1,)), ((), ()))
    down = (((0,), (0,)), ((), ()))
    all_grad = grad[...].reshape(LEN, HD)
    for i in range(LEN // step - 1, -1, -1):
        low, high = i * step, (i + 1) * step
        q = query[0, low:high]
        g = all_grad[low:high]
        k = key[0, :high]
        v = value[0, :high]
        scores = lax.dot_general(q, k, across, preferred_element_type=jnp.float32) * scale
        place_q = low + lax.broadcasted_iota(jnp.int32, (step, high), 0)
        place_k = lax.broadcasted_iota(jnp.int32, (step, high), 1)
        visible = (place_k <= place_q) & (seg_col[0, low:high] == seg_row[0, :, :high])
        scores = jnp.where(visible, scores, masked_fill)
        peak = jnp.max(scores, axis=1, keepdims=True)
        exponent = jnp.exp(scores - peak)
        prob = exponent * (1.0 / jnp.sum(exponent, axis=1, keepdims=True))
        pgrad = lax.dot_general(g, v, across, preferred_element_type=jnp.float32)
        delta = jnp.sum(prob * pgrad, axis=1, keepdims=True)
        sgrad = (prob * (pgrad - delta)).astype(jnp.bfloat16)
        half = prob.astype(jnp.bfloat16)
        dquery[0, low:high] = (scale * jnp.dot(sgrad, k, preferred_element_type=jnp.float32)).astype(jnp.bfloat16)
        kpart = lax.dot_general(sgrad, q, down, preferred_element_type=jnp.float32)
        vpart = lax.dot_general(half, g, down, preferred_element_type=jnp.float32)
        if i == LEN // step - 1:
            kacc[...] = kpart
            vacc[...] = vpart
        else:
            kacc[:high] += kpart
            vacc[:high] += vpart
    dkey[0] = (scale * kacc[...]).astype(jnp.bfloat16)
    dvalue[0] = vacc[...].astype(jnp.bfloat16)


def attend(queries, keys, values, grads, segments):
    flat = pl.BlockSpec((1, LEN, HD), lambda b, h: (b, 0, h))
    return pl.pallas_call(
        attend_kernel,
        grid=(2, 2),
        out_shape=[jax.ShapeDtypeStruct((2, LEN, 256), jnp.bfloat16)] * 3,
        in_specs=[
            flat,
            flat,
            flat,
            pl.BlockSpec((16, 1, 64, HD), lambda b, h: (0, b, 0, h)),
            pl.BlockSpec((1, LEN, 1), lambda b, h: (b, 0, 0)),
            pl.BlockSpec((1, 1, LEN), lambda b, h: (b, 0, 0)),
        ],
        out_specs=[flat, flat, flat],
        scratch_shapes=[pltpu.VMEM((LEN, HD), jnp.float32)] * 2,
        compiler_params=pltpu.CompilerParams(vmem_limit_bytes=48 * MIB),
        cost_estimate=pl.CostEstimate(flops=5 * 10**9, bytes_accessed=8 * MIB, transcendentals=4 * 10**6),
        name="attend",
    )(queries, keys, values, grads, segments.reshape(2, LEN, 1), segments.reshape(2, 1, LEN))


def feed_forward(case, ffn_hidden, out_grad, butterfly, up_weight, down_weight):
    bits = Bits(butterfly)
    count = {0: 4, 3: 1}.get(case, 2)
    tensor = lax.axis_index("tensor")
    seq = lax.axis_index("seq")
    zpos = tensor & 3
    qpos = ((seq >> 2) << 1) | (seq & 1)
    grad = out_grad.reshape(ROWS, D)

    slot_ids = jnp.arange(count, dtype=jnp.int32)
    if case == 0:
        cosets = slot_ids[None, :]
    else:
        targets = zpos ^ jnp.arange(4, dtype=jnp.int32)
        if case == 3:
            cosets = targets[:, None]
        else:
            cosets = 2 * ((targets >> (1 if case == 2 else 0)) & 1)[:, None] + slot_ids[None, :]
    rank_ids = jnp.arange(NNZ, dtype=jnp.int32)
    source = bits.block(
        jnp.broadcast_to(cosets[:, :, None], cosets.shape + (NNZ,)),
        jnp.broadcast_to(rank_ids[None, None, :], cosets.shape + (NNZ,)),
    ).reshape(-1)
    chunks = list(gather_columns(grad, source, cosets.shape[0], count))

    ranks = bits.rank(butterfly)
    match = ranks[:, None, :] == jnp.arange(NNZ, dtype=jnp.int32)[None, :, None]
    order = jnp.sum(jnp.where(match, jnp.arange(NNZ, dtype=jnp.int32)[None, None, :], 0), axis=2, dtype=jnp.int32)
    packed = pack_weights(down_weight, up_weight, order, 2 * qpos)
    shares = [
        lax.dynamic_slice_in_dim(ffn_hidden, 8 * (target_of(tensor, case, piece) >> 2), 8, 0) for piece in range(4)
    ]
    tied = tie(packed, *shares, *chunks)
    packed, shares, chunks = tied[0], tied[1:5], list(tied[5:])
    if case == 0:
        chunks = chunks * 4
    gathered = jnp.stack([send_piece(packed, case, piece) for piece in range(4)])
    hidden = [send_piece(shares[piece], case, piece) for piece in range(4)]
    grads = [chunks[0]] + [flip(chunks[d], "tensor", d) for d in (1, 2, 3)]

    right = flip(gathered, "seq", 4)
    left = flip(gathered, "seq", 12)
    right, left, hidden[0], hidden[1], hidden[3], grads[1] = tie(right, left, hidden[0], hidden[1], hidden[3], grads[1])
    across_a = flip(left[:2], "seq", 4)
    across_b = flip(right[2:], "seq", 12)
    across_a, across_b, hidden[2], grads[2], grads[3] = tie(across_a, across_b, hidden[2], grads[2], grads[3])
    mine = [gathered, right, left, across_a, across_b]
    weights = mine + [flip(part, "seq", 1) for part in mine]

    slopes = [
        gelu_slope(part.astype(jnp.float32)).astype(jnp.bfloat16).reshape(8 * 64, 4 * FB) for part in hidden
    ]

    holders = jnp.stack([source_of(tensor, case, piece) for piece in range(4)]).astype(jnp.int32)
    own_blocks = holders[:, None] * 4 + jnp.arange(4, dtype=jnp.int32)[None, :]
    own_slots = bits.coset(own_blocks) & (count - 1)
    present = jnp.any(own_slots[:, :, None] == slot_ids[None, None, :], axis=1).astype(jnp.int32)
    table = jnp.concatenate([jnp.stack([zpos, qpos]).astype(jnp.int32), present.reshape(-1)])
    lanes = jnp.broadcast_to(own_slots[:, None, :, None], (4, 1, 4, FB)).reshape(4, 1, 4 * FB)
    parts = ffn(table, lanes, weights, slopes, grads, count)

    parts = [parts[0]] + [flip(parts[d], "tensor", d) for d in (1, 2, 3)]
    blocks = jnp.arange(NBLK, dtype=jnp.int32)
    places = bits.coset(blocks) * NNZ + bits.rank(blocks)
    return combine(case, jnp.concatenate([places, zpos.reshape(1).astype(jnp.int32)]), grad, parts)


def per_device(
    queries, keys, values, ffn_hidden, out_grad, butterfly, segments, up_weight, down_weight
):
    heads = lax.switch(
        Bits(butterfly).case,
        [functools.partial(feed_forward, case) for case in range(6)],
        ffn_hidden,
        out_grad,
        butterfly,
        up_weight,
        down_weight,
    )
    arrived = lax.all_to_all(heads, "seq", split_axis=0, concat_axis=0, tiled=True)
    return tuple(attend(queries, keys, values, arrived.reshape(16, 2, 64, 256), segments))


def solution(mesh):
    placed = (
        P("tensor", None, "seq"),
        P("tensor", None, "seq"),
        P("tensor", None, "seq"),
        P(None, "seq", "tensor"),
        P("tensor", "seq", None),
        P("tensor", None),
        P("tensor", None),
        P("tensor", None, None, None),
        P("tensor", None, None, None),
    )
    return jax.shard_map(
        per_device,
        mesh=mesh,
        in_specs=placed,
        out_specs=(P("tensor", None, "seq"), P("tensor", None, "seq"), P("tensor", None, "seq")),
        check_vma=False,
    )
```

```python
import functools
import math

import jax
import jax.numpy as jnp
from jax import lax
from jax.experimental import pallas as pl
from jax.experimental.pallas import tpu as pltpu
from jax.sharding import PartitionSpec as P

D = 4096
HD = 128
FF = 11264
NBLK = 64
NNZ = 16
DB = 64
FB = 176
LEN = 1024
ROWS = 128
MIB = 1 << 20

masked_fill = -1e30


def gelu_slope(hidden):
    cumulative = 0.5 * (1.0 + jax.scipy.special.erf(hidden * 0.7071067811865476))
    return cumulative + hidden * jnp.exp(-0.5 * hidden * hidden) * 0.3989422804014327


def flip(array, axis, mask):
    return lax.ppermute(array, axis, [(i, i ^ mask) for i in range(16)])


def swapped_index(tensor, kind):
    if kind not in (2, 3):
        return tensor
    low, high = tensor & 1, (tensor >> kind) & 1
    return (tensor & ~((1 << kind) | 1)) | (low << kind) | high


def blocks_of(tensor, kind):
    local = jnp.arange(4, dtype=jnp.int32)
    holders = jnp.stack([swapped_index(tensor ^ (4 * piece), kind) for piece in range(4)]).astype(jnp.int32)[:, None]
    if kind == 4:
        return (holders ^ (local >> 1)[None, :]) * 4 + 2 * (tensor & 1) + (local & 1)[None, :]
    return holders * 4 + local[None, :]


def align(kind, packed, hidden):
    if kind < 2:
        return packed, hidden
    if kind < 4:
        pairs = [(i, swapped_index(i, kind)) for i in range(16)]
        return lax.ppermute(packed, "tensor", pairs), lax.ppermute(hidden, "tensor", pairs)
    low = lax.axis_index("tensor") & 1
    results = []
    for array, axis in ((packed, 1), (hidden, 2)):
        half = array.shape[axis] // 2
        own = lax.dynamic_slice_in_dim(array, half * low, half, axis)
        other = flip(lax.dynamic_slice_in_dim(array, half * (1 - low), half, axis), "tensor", 1)
        results.append(jnp.concatenate([own, other], axis=axis))
    return tuple(results)


def tie(*arrays):
    return lax.optimization_barrier(arrays)


class Bits:
    def __init__(self, butterfly):
        row = butterfly[0]
        span = lax.reduce(row ^ row[0], jnp.int32(0), lax.bitwise_or, (0,))
        missing = 63 & ~span
        zpart = missing & 12
        swapped = jnp.where((missing & 16) != 0, 16, jnp.where((missing & 32) != 0, 32, 2))
        by_swap = jnp.where(swapped == 16, 2, jnp.where(swapped == 32, 3, 4))
        by_z = jnp.where(zpart == 8, 8, 4)
        self.missing = missing
        self.high = jnp.where(zpart == 0, swapped, by_z)
        self.low = missing ^ self.high
        self.kind = jnp.where(zpart == 0, by_swap, by_z >> 3)

    def coset(self, block):
        return 2 * ((block & self.high) != 0).astype(jnp.int32) + ((block & self.low) != 0).astype(jnp.int32)

    def rank(self, block):
        total = jnp.zeros_like(block)
        below = jnp.int32(0)
        for i in range(6):
            kept = 1 - ((self.missing >> i) & 1)
            total = total + ((((block >> i) & 1) * kept) << below)
            below = below + kept
        return total

    def block(self, coset, rank):
        total = jnp.zeros_like(rank)
        below = jnp.int32(0)
        for i in range(6):
            gone = (self.missing >> i) & 1
            of_coset = jnp.where(self.high == (1 << i), coset >> 1, coset & 1)
            bit = jnp.where(gone == 1, of_coset, (rank >> below) & 1)
            total = total | (bit << i)
            below = below + 1 - gone
        return total


def half_tiles(load, first, second):
    left = pltpu.roll(load(first), 64 * (first & 1), 1)
    right = pltpu.roll(load(second), 64 * (1 - (second & 1)), 1)
    lane = lax.broadcasted_iota(jnp.int32, left.shape, 1)
    return jnp.where(lane < 64, left, right)


def gather_columns_kernel(count, table, grad, *outs):
    def load(block):
        start = pl.multiple_of((block >> 1) * 128, 128)
        return grad[:, pl.ds(start, 128)].astype(jnp.float32)

    for target, out in enumerate(outs):
        for slot in range(count):

            def tile(i, carry, target=target, out=out, slot=slot):
                at = (target * count + slot) * 16 + 2 * i
                value = half_tiles(load, table[at], table[at + 1])
                out[slot, :, pl.ds(pl.multiple_of(i * 128, 128), 128)] = value.astype(jnp.bfloat16)
                return carry

            lax.fori_loop(0, 8, tile, 0)


def gather_columns(grad, table, targets, count):
    smem = pl.BlockSpec(memory_space=pltpu.SMEM)
    vmem = pl.BlockSpec(memory_space=pltpu.VMEM)
    return pl.pallas_call(
        functools.partial(gather_columns_kernel, count),
        out_shape=[jax.ShapeDtypeStruct((count, ROWS, 1024), jnp.bfloat16)] * targets,
        in_specs=[smem, vmem],
        out_specs=[vmem] * targets,
        compiler_params=pltpu.CompilerParams(vmem_limit_bytes=24 * MIB),
        name="gather_columns",
    )(table, grad)


def pack_weights_kernel(order, *refs):
    out = refs[16]
    eye = (
        lax.broadcasted_iota(jnp.int32, (2 * DB, 2 * DB), 0) == lax.broadcasted_iota(jnp.int32, (2 * DB, 2 * DB), 1)
    ).astype(jnp.bfloat16)
    for kind in range(2):
        for local in range(4):
            pair = [refs[(kind * 4 + local) * 2 + rank][0, 0] for rank in range(2)]
            both = jnp.concatenate(pair, axis=0)
            turned = lax.dot_general(both, eye, (((0,), (0,)), ((), ())), preferred_element_type=jnp.float32)
            out[kind, local * FB:(local + 1) * FB] = turned.astype(jnp.bfloat16)


def pack_weights(down, up, order, first):
    def spec(local, rank):
        return pl.BlockSpec((1, 1, DB, FB), lambda i, order: (local, order[local * 2 + rank], 0, 0))

    grid = pltpu.PrefetchScalarGridSpec(
        num_scalar_prefetch=1,
        grid=(1,),
        in_specs=[spec(local, rank) for local in range(4) for rank in range(2)] * 2,
        out_specs=pl.BlockSpec((2, 4 * FB, 2 * DB), lambda i, order: (0, 0, 0)),
    )
    chosen = lax.dynamic_slice_in_dim(order, first, 2, 1).reshape(8)
    return pl.pallas_call(
        pack_weights_kernel,
        grid_spec=grid,
        out_shape=jax.ShapeDtypeStruct((2, 4 * FB, 2 * DB), jnp.bfloat16),
        name="pack_weights",
    )(chosen, *[down] * 8, *[up] * 8)


WEIGHT_PARTS = ((0, 0, 4), (2, 0, 4), (6, 0, 4), (4, 0, 2), (4, 2, 4), (1, 0, 4), (3, 0, 4), (7, 0, 4), (5, 0, 2), (5, 2, 4))


def ffn_kernel(count, table, slots, *refs):
    weights, slopes, grads = refs[:10], refs[10:14], refs[14:18]
    outs = refs[18:22]
    wbuf, sbuf, gbuf, acc, wsem, ssem, gsem = refs[22:]
    zpos, qpos = table[0], table[1]
    early, weight_copies = [], [[], [], [], []]
    for z in range(4):
        early.append(pltpu.make_async_copy(grads[z], gbuf.at[:, z], gsem.at[z]))
        for y in range(4):
            source = slopes[y].at[pl.ds(pl.multiple_of((zpos ^ z) * ROWS, ROWS), ROWS)]
            early.append(pltpu.make_async_copy(source, sbuf.at[y, z], ssem.at[y * 4 + z]))
    for i, (mask, first, last) in enumerate(WEIGHT_PARTS):
        columns = pl.ds(pl.multiple_of((qpos ^ mask) * 2 * DB, 2 * DB), 2 * DB)
        for y in range(first, last):
            weight_copies[y].append(
                pltpu.make_async_copy(weights[i].at[y - first], wbuf.at[y, :, :, columns], wsem.at[i * 4 + y])
            )
    for copy in early + weight_copies[0] + weight_copies[1] + weight_copies[2] + weight_copies[3]:
        copy.start()
    acc[...] = jnp.zeros_like(acc)
    for copy in early:
        copy.wait()

    for y in range(4):
        for copy in weight_copies[y]:
            copy.wait()

        def one_slot(slot, carry, y=y):
            @pl.when(table[2 + y * count + slot] != 0)
            def _():
                grad = gbuf[slot].reshape(4 * ROWS, 1024)
                hidden = lax.dot_general(
                    grad, wbuf[y, 0], (((1,), (1,)), ((), ())), preferred_element_type=jnp.float32
                )
                hidden = hidden * sbuf[y].reshape(4 * ROWS, 4 * FB).astype(jnp.float32)
                hidden = jnp.where(slots[y] == slot, hidden, 0.0).astype(jnp.bfloat16)
                acc[slot] += jnp.dot(hidden, wbuf[y, 1], preferred_element_type=jnp.float32)

            return carry

        lax.fori_loop(0, count, one_slot, 0)
    for z in range(4):
        outs[z][...] = acc[:, z * ROWS:(z + 1) * ROWS].astype(jnp.bfloat16)


def ffn(table, slots, weights, slopes, grads, count):
    hbm = pl.BlockSpec(memory_space=pl.ANY)
    vmem = pl.BlockSpec(memory_space=pltpu.VMEM)
    return pl.pallas_call(
        functools.partial(ffn_kernel, count),
        out_shape=[jax.ShapeDtypeStruct((count, ROWS, 1024), jnp.bfloat16)] * 4,
        in_specs=[pl.BlockSpec(memory_space=pltpu.SMEM), vmem] + [hbm] * 18,
        out_specs=[vmem] * 4,
        scratch_shapes=[
            pltpu.VMEM((4, 2, 4 * FB, 16 * DB), jnp.bfloat16),
            pltpu.VMEM((4, 4, ROWS, 4 * FB), jnp.bfloat16),
            pltpu.VMEM((count, 4, ROWS, 1024), jnp.bfloat16),
            pltpu.VMEM((count, 4 * ROWS, 1024), jnp.float32),
            pltpu.SemaphoreType.DMA((40,)),
            pltpu.SemaphoreType.DMA((16,)),
            pltpu.SemaphoreType.DMA((4,)),
        ],
        compiler_params=pltpu.CompilerParams(vmem_limit_bytes=52 * MIB),
        cost_estimate=pl.CostEstimate(flops=6 * 10**9, bytes_accessed=24 * MIB, transcendentals=0),
        name="ffn",
    )(table, slots, *weights, *slopes, *grads)


def combine_kernel(table, grad, p0, p1, p2, p3, out, whole):
    side = table[64]
    for slot in range(2):
        own, near, far, last = [part[slot].astype(jnp.float32) for part in (p0, p1, p2, p3)]
        pick = jnp.full(near.shape, table[65], jnp.int32) != 0
        whole[2 * side + slot] = own + jnp.where(pick, near, far)
        whole[2 * (1 - side) + slot] = last + jnp.where(pick, far, near)

    def load(position):
        start = pl.multiple_of(((position & 15) >> 1) * 128, 128)
        return whole[position >> 4, :, pl.ds(start, 128)]

    def dest(k, carry):
        for half in range(2):
            tile = 2 * k + half
            value = half_tiles(load, table[2 * tile], table[2 * tile + 1])
            own = grad[:, pl.ds(pl.multiple_of(tile * 128, 128), 128)].astype(jnp.float32)
            out[k, :, half * 128:(half + 1) * 128] = (own + value).astype(jnp.bfloat16)
        return carry

    lax.fori_loop(0, 16, dest, 0)


def combine(table, grad, parts):
    vmem = pl.BlockSpec(memory_space=pltpu.VMEM)
    return pl.pallas_call(
        combine_kernel,
        out_shape=jax.ShapeDtypeStruct((16, ROWS, 256), jnp.bfloat16),
        in_specs=[pl.BlockSpec(memory_space=pltpu.SMEM)] + [vmem] * 5,
        out_specs=vmem,
        scratch_shapes=[pltpu.VMEM((4, ROWS, 1024), jnp.float32)],
        compiler_params=pltpu.CompilerParams(vmem_limit_bytes=24 * MIB),
        cost_estimate=pl.CostEstimate(flops=10**6, bytes_accessed=2 * MIB, transcendentals=0),
        name="combine",
    )(table, grad, *parts)


def attend_kernel(query, key, value, grad, seg_col, seg_row, dquery, dkey, dvalue, kacc, vacc):
    scale = 1.0 / math.sqrt(HD)
    step = 256
    across = (((1,), (1,)), ((), ()))
    down = (((0,), (0,)), ((), ()))
    all_grad = grad[...].reshape(LEN, HD)
    for i in range(LEN // step - 1, -1, -1):
        low, high = i * step, (i + 1) * step
        q = query[0, low:high]
        g = all_grad[low:high]
        k = key[0, :high]
        v = value[0, :high]
        scores = lax.dot_general(q, k, across, preferred_element_type=jnp.float32) * scale
        place_q = low + lax.broadcasted_iota(jnp.int32, (step, high), 0)
        place_k = lax.broadcasted_iota(jnp.int32, (step, high), 1)
        visible = (place_k <= place_q) & (seg_col[0, low:high] == seg_row[0, :, :high])
        scores = jnp.where(visible, scores, masked_fill)
        peak = jnp.max(scores, axis=1, keepdims=True)
        exponent = jnp.exp(scores - peak)
        prob = exponent * (1.0 / jnp.sum(exponent, axis=1, keepdims=True))
        pgrad = lax.dot_general(g, v, across, preferred_element_type=jnp.float32)
        delta = jnp.sum(prob * pgrad, axis=1, keepdims=True)
        sgrad = (prob * (pgrad - delta)).astype(jnp.bfloat16)
        half = prob.astype(jnp.bfloat16)
        dquery[0, low:high] = (scale * jnp.dot(sgrad, k, preferred_element_type=jnp.float32)).astype(jnp.bfloat16)
        kpart = lax.dot_general(sgrad, q, down, preferred_element_type=jnp.float32)
        vpart = lax.dot_general(half, g, down, preferred_element_type=jnp.float32)
        if i == LEN // step - 1:
            kacc[...] = kpart
            vacc[...] = vpart
        else:
            kacc[:high] += kpart
            vacc[:high] += vpart
    dkey[0] = (scale * kacc[...]).astype(jnp.bfloat16)
    dvalue[0] = vacc[...].astype(jnp.bfloat16)


def attend(queries, keys, values, grads, segments):
    flat = pl.BlockSpec((1, LEN, HD), lambda b, h: (b, 0, h))
    return pl.pallas_call(
        attend_kernel,
        grid=(2, 2),
        out_shape=[jax.ShapeDtypeStruct((2, LEN, 256), jnp.bfloat16)] * 3,
        in_specs=[
            flat,
            flat,
            flat,
            pl.BlockSpec((16, 1, 64, HD), lambda b, h: (0, b, 0, h)),
            pl.BlockSpec((1, LEN, 1), lambda b, h: (b, 0, 0)),
            pl.BlockSpec((1, 1, LEN), lambda b, h: (b, 0, 0)),
        ],
        out_specs=[flat, flat, flat],
        scratch_shapes=[pltpu.VMEM((LEN, HD), jnp.float32)] * 2,
        compiler_params=pltpu.CompilerParams(vmem_limit_bytes=48 * MIB),
        cost_estimate=pl.CostEstimate(flops=5 * 10**9, bytes_accessed=8 * MIB, transcendentals=4 * 10**6),
        name="attend",
    )(queries, keys, values, grads, segments.reshape(2, LEN, 1), segments.reshape(2, 1, LEN))


def per_device(
    queries, keys, values, ffn_hidden, out_grad, butterfly, segments, up_weight, down_weight
):
    bits = Bits(butterfly)
    tensor = lax.axis_index("tensor")
    seq = lax.axis_index("seq")
    zpos = tensor & 3
    qpos = ((seq >> 2) << 1) | (seq & 1)
    high_z = (bits.kind == 1).astype(jnp.int32)
    side = (zpos >> high_z) & 1

    ranks = bits.rank(butterfly)
    match = ranks[:, None, :] == jnp.arange(NNZ, dtype=jnp.int32)[None, :, None]
    order = jnp.sum(jnp.where(match, jnp.arange(NNZ, dtype=jnp.int32)[None, None, :], 0), axis=2, dtype=jnp.int32)
    packed = pack_weights(down_weight, up_weight, order, 2 * qpos)

    packed, hidden = lax.switch(
        jnp.maximum(bits.kind - 1, 0), [functools.partial(align, kind) for kind in range(1, 5)], packed, ffn_hidden
    )

    place = jnp.arange(NBLK, dtype=jnp.int32)
    source = bits.block((place >> 4) ^ (2 * side), place & 15)
    from_y = [packed] + [flip(packed, "tensor", 4 * d) for d in (1, 2, 3)]
    own_side, other_side = gather_columns(out_grad.reshape(ROWS, D), source, 2, 2)
    chunks = [
        jnp.where(high_z == 1, own_side, other_side),
        jnp.where(high_z == 1, other_side, own_side),
        other_side,
    ]
    ypos = tensor >> 2
    shares = [lax.dynamic_slice_in_dim(hidden, 8 * (ypos ^ d), 8, 0) for d in range(4)]
    gathered = jnp.stack(from_y)
    tied = tie(gathered, *chunks, *shares)
    gathered, chunks, shares = tied[0], tied[1:4], tied[4:]
    hidden = [shares[0]] + [flip(shares[d], "tensor", 4 * d) for d in (1, 2, 3)]
    grads = [flip(chunks[d - 1], "tensor", d) for d in (1, 2, 3)]

    right = flip(gathered, "seq", 4)
    left = flip(gathered, "seq", 12)
    right, left, hidden[1], hidden[3], grads[0] = tie(right, left, hidden[1], hidden[3], grads[0])
    across_a = flip(left[:2], "seq", 4)
    across_b = flip(right[2:], "seq", 12)
    across_a, across_b, hidden[2], grads[1], grads[2] = tie(across_a, across_b, hidden[2], grads[1], grads[2])
    mine = [gathered, right, left, across_a, across_b]
    weights = mine + [flip(part, "seq", 1) for part in mine]
    slopes = [
        gelu_slope(part.astype(jnp.float32)).astype(jnp.bfloat16).reshape(8 * 64, 4 * FB) for part in hidden
    ]

    own_blocks = lax.dynamic_index_in_dim(
        jnp.stack([blocks_of(tensor, kind) for kind in range(5)]), bits.kind, 0, keepdims=False
    )
    own_slots = bits.coset(own_blocks) & 1
    present = jnp.any(own_slots[:, :, None] == jnp.arange(2, dtype=jnp.int32), axis=1).astype(jnp.int32)
    table = jnp.concatenate([jnp.stack([zpos, qpos]).astype(jnp.int32), present.reshape(-1)])
    lanes = jnp.broadcast_to(own_slots[:, None, :, None], (4, 1, 4, FB)).reshape(4, 1, 4 * FB)
    parts = ffn(table, lanes, weights, slopes, [own_side] + grads, 2)

    places = bits.coset(place) * NNZ + bits.rank(place)
    table = jnp.concatenate([places, jnp.stack([side, high_z]).astype(jnp.int32)])
    parts = [parts[0]] + [flip(parts[d], "tensor", d) for d in (1, 2, 3)]
    heads = combine(table, out_grad.reshape(ROWS, D), parts)
    arrived = lax.all_to_all(heads, "seq", split_axis=0, concat_axis=0, tiled=True)
    return tuple(attend(queries, keys, values, arrived.reshape(16, 2, 64, 256), segments))


def solution(mesh):
    placed = (
        P("tensor", None, "seq"),
        P("tensor", None, "seq"),
        P("tensor", None, "seq"),
        P(None, "seq", "tensor"),
        P("tensor", "seq", None),
        P("tensor", None),
        P("tensor", None),
        P("tensor", None, None, None),
        P("tensor", None, None, None),
    )
    return jax.shard_map(
        per_device,
        mesh=mesh,
        in_specs=placed,
        out_specs=(P("tensor", None, "seq"), P("tensor", None, "seq"), P("tensor", None, "seq")),
        check_vma=False,
    )
```

```python
import functools
import math

import jax
import jax.numpy as jnp
from jax import lax
from jax.experimental import pallas as pl
from jax.experimental.pallas import tpu as pltpu
from jax.sharding import PartitionSpec as P

D = 4096
HD = 128
FF = 11264
NBLK = 64
NNZ = 16
DB = 64
FB = 176
LEN = 1024
ROWS = 128
MIB = 1 << 20

masked_fill = -1e30


def gelu_slope(hidden):
    cumulative = 0.5 * (1.0 + jax.scipy.special.erf(hidden * 0.7071067811865476))
    return cumulative + hidden * jnp.exp(-0.5 * hidden * hidden) * 0.3989422804014327


def flip(array, axis, mask):
    return lax.ppermute(array, axis, [(i, i ^ mask) for i in range(16)])


def swapped_index(tensor, kind):
    if kind not in (2, 3):
        return tensor
    low, high = tensor & 1, (tensor >> kind) & 1
    return (tensor & ~((1 << kind) | 1)) | (low << kind) | high


def blocks_of(tensor, kind):
    local = jnp.arange(4, dtype=jnp.int32)
    holders = jnp.stack([swapped_index(tensor ^ (4 * piece), kind) for piece in range(4)]).astype(jnp.int32)[:, None]
    if kind == 4:
        return (holders ^ (local >> 1)[None, :]) * 4 + 2 * (tensor & 1) + (local & 1)[None, :]
    return holders * 4 + local[None, :]


def align(kind, packed, hidden):
    if kind < 2:
        return packed, hidden
    if kind < 4:
        pairs = [(i, swapped_index(i, kind)) for i in range(16)]
        return lax.ppermute(packed, "tensor", pairs), lax.ppermute(hidden, "tensor", pairs)
    low = lax.axis_index("tensor") & 1
    results = []
    for array, axis in ((packed, 1), (hidden, 2)):
        half = array.shape[axis] // 2
        own = lax.dynamic_slice_in_dim(array, half * low, half, axis)
        other = flip(lax.dynamic_slice_in_dim(array, half * (1 - low), half, axis), "tensor", 1)
        results.append(jnp.concatenate([own, other], axis=axis))
    return tuple(results)


def tie(*arrays):
    return lax.optimization_barrier(arrays)


class Bits:
    def __init__(self, butterfly):
        row = butterfly[0]
        span = lax.reduce(row ^ row[0], jnp.int32(0), lax.bitwise_or, (0,))
        missing = 63 & ~span
        zpart = missing & 12
        swapped = jnp.where((missing & 16) != 0, 16, jnp.where((missing & 32) != 0, 32, 2))
        by_swap = jnp.where(swapped == 16, 2, jnp.where(swapped == 32, 3, 4))
        by_z = jnp.where(zpart == 8, 8, 4)
        self.missing = missing
        self.high = jnp.where(zpart == 0, swapped, by_z)
        self.low = missing ^ self.high
        self.kind = jnp.where(zpart == 0, by_swap, by_z >> 3)

    def coset(self, block):
        return 2 * ((block & self.high) != 0).astype(jnp.int32) + ((block & self.low) != 0).astype(jnp.int32)

    def rank(self, block):
        total = jnp.zeros_like(block)
        below = jnp.int32(0)
        for i in range(6):
            kept = 1 - ((self.missing >> i) & 1)
            total = total + ((((block >> i) & 1) * kept) << below)
            below = below + kept
        return total

    def block(self, coset, rank):
        total = jnp.zeros_like(rank)
        below = jnp.int32(0)
        for i in range(6):
            gone = (self.missing >> i) & 1
            of_coset = jnp.where(self.high == (1 << i), coset >> 1, coset & 1)
            bit = jnp.where(gone == 1, of_coset, (rank >> below) & 1)
            total = total | (bit << i)
            below = below + 1 - gone
        return total


def half_tiles(load, first, second):
    left = pltpu.roll(load(first), 64 * (first & 1), 1)
    right = pltpu.roll(load(second), 64 * (1 - (second & 1)), 1)
    lane = lax.broadcasted_iota(jnp.int32, left.shape, 1)
    return jnp.where(lane < 64, left, right)


def gather_columns_kernel(count, table, grad, *outs):
    def load(block):
        start = pl.multiple_of((block >> 1) * 128, 128)
        return grad[:, pl.ds(start, 128)].astype(jnp.float32)

    for target, out in enumerate(outs):
        for slot in range(count):

            def tile(i, carry, target=target, out=out, slot=slot):
                at = (target * count + slot) * 16 + 2 * i
                value = half_tiles(load, table[at], table[at + 1])
                out[slot, :, pl.ds(pl.multiple_of(i * 128, 128), 128)] = value.astype(jnp.bfloat16)
                return carry

            lax.fori_loop(0, 8, tile, 0)


def gather_columns(grad, table, targets, count):
    smem = pl.BlockSpec(memory_space=pltpu.SMEM)
    vmem = pl.BlockSpec(memory_space=pltpu.VMEM)
    return pl.pallas_call(
        functools.partial(gather_columns_kernel, count),
        out_shape=[jax.ShapeDtypeStruct((count, ROWS, 1024), jnp.bfloat16)] * targets,
        in_specs=[smem, vmem],
        out_specs=[vmem] * targets,
        compiler_params=pltpu.CompilerParams(vmem_limit_bytes=24 * MIB),
        name="gather_columns",
    )(table, grad)


def pack_weights_kernel(order, *refs):
    out = refs[16]
    eye = (
        lax.broadcasted_iota(jnp.int32, (2 * DB, 2 * DB), 0) == lax.broadcasted_iota(jnp.int32, (2 * DB, 2 * DB), 1)
    ).astype(jnp.bfloat16)
    for kind in range(2):
        for local in range(4):
            pair = [refs[(kind * 4 + local) * 2 + rank][0, 0] for rank in range(2)]
            both = jnp.concatenate(pair, axis=0)
            turned = lax.dot_general(both, eye, (((0,), (0,)), ((), ())), preferred_element_type=jnp.float32)
            out[kind, local * FB:(local + 1) * FB] = turned.astype(jnp.bfloat16)


def pack_weights(down, up, order, first):
    def spec(local, rank):
        return pl.BlockSpec((1, 1, DB, FB), lambda i, order: (local, order[local * 2 + rank], 0, 0))

    grid = pltpu.PrefetchScalarGridSpec(
        num_scalar_prefetch=1,
        grid=(1,),
        in_specs=[spec(local, rank) for local in range(4) for rank in range(2)] * 2,
        out_specs=pl.BlockSpec((2, 4 * FB, 2 * DB), lambda i, order: (0, 0, 0)),
    )
    chosen = lax.dynamic_slice_in_dim(order, first, 2, 1).reshape(8)
    return pl.pallas_call(
        pack_weights_kernel,
        grid_spec=grid,
        out_shape=jax.ShapeDtypeStruct((2, 4 * FB, 2 * DB), jnp.bfloat16),
        name="pack_weights",
    )(chosen, *[down] * 8, *[up] * 8)


WEIGHT_PARTS = ((0, 0, 4), (2, 0, 4), (6, 0, 4), (4, 0, 2), (4, 2, 4), (1, 0, 4), (3, 0, 4), (7, 0, 4), (5, 0, 2), (5, 2, 4))


def ffn_kernel(count, table, slots, *refs):
    weights, slopes, grads = refs[:10], refs[10:14], refs[14:18]
    outs = refs[18:22]
    wbuf, sbuf, gbuf, acc, wsem, ssem, gsem = refs[22:]
    zpos, qpos = table[0], table[1]
    early, weight_copies = [], [[], [], [], []]
    for z in range(4):
        early.append(pltpu.make_async_copy(grads[z], gbuf.at[:, z], gsem.at[z]))
        for y in range(4):
            source = slopes[y].at[pl.ds(pl.multiple_of((zpos ^ z) * ROWS, ROWS), ROWS)]
            early.append(pltpu.make_async_copy(source, sbuf.at[y, z], ssem.at[y * 4 + z]))
    for i, (mask, first, last) in enumerate(WEIGHT_PARTS):
        columns = pl.ds(pl.multiple_of((qpos ^ mask) * 2 * DB, 2 * DB), 2 * DB)
        for y in range(first, last):
            weight_copies[y].append(
                pltpu.make_async_copy(weights[i].at[y - first], wbuf.at[y, :, :, columns], wsem.at[i * 4 + y])
            )
    for copy in early + weight_copies[0] + weight_copies[1] + weight_copies[2] + weight_copies[3]:
        copy.start()
    acc[...] = jnp.zeros_like(acc)
    for copy in early:
        copy.wait()

    for y in range(4):
        for copy in weight_copies[y]:
            copy.wait()

        def one_slot(slot, carry, y=y):
            @pl.when(table[2 + y * count + slot] != 0)
            def _():
                grad = gbuf[slot].reshape(4 * ROWS, 1024)
                hidden = lax.dot_general(
                    grad, wbuf[y, 0], (((1,), (1,)), ((), ())), preferred_element_type=jnp.float32
                )
                hidden = hidden * sbuf[y].reshape(4 * ROWS, 4 * FB).astype(jnp.float32)
                hidden = jnp.where(slots[y] == slot, hidden, 0.0).astype(jnp.bfloat16)
                acc[slot] += jnp.dot(hidden, wbuf[y, 1], preferred_element_type=jnp.float32)

            return carry

        lax.fori_loop(0, count, one_slot, 0)
    for z in range(4):
        outs[z][...] = acc[:, z * ROWS:(z + 1) * ROWS].astype(jnp.bfloat16)


def ffn(table, slots, weights, slopes, grads, count):
    hbm = pl.BlockSpec(memory_space=pl.ANY)
    vmem = pl.BlockSpec(memory_space=pltpu.VMEM)
    return pl.pallas_call(
        functools.partial(ffn_kernel, count),
        out_shape=[jax.ShapeDtypeStruct((count, ROWS, 1024), jnp.bfloat16)] * 4,
        in_specs=[pl.BlockSpec(memory_space=pltpu.SMEM), vmem] + [hbm] * 18,
        out_specs=[vmem] * 4,
        scratch_shapes=[
            pltpu.VMEM((4, 2, 4 * FB, 16 * DB), jnp.bfloat16),
            pltpu.VMEM((4, 4, ROWS, 4 * FB), jnp.bfloat16),
            pltpu.VMEM((count, 4, ROWS, 1024), jnp.bfloat16),
            pltpu.VMEM((count, 4 * ROWS, 1024), jnp.float32),
            pltpu.SemaphoreType.DMA((40,)),
            pltpu.SemaphoreType.DMA((16,)),
            pltpu.SemaphoreType.DMA((4,)),
        ],
        compiler_params=pltpu.CompilerParams(vmem_limit_bytes=52 * MIB),
        cost_estimate=pl.CostEstimate(flops=6 * 10**9, bytes_accessed=24 * MIB, transcendentals=0),
        name="ffn",
    )(table, slots, *weights, *slopes, *grads)


def combine_kernel(table, grad, p0, p1, p2, p3, out, whole):
    side = table[64]
    for slot in range(2):
        own, near, far, last = [part[slot].astype(jnp.float32) for part in (p0, p1, p2, p3)]
        pick = jnp.full(near.shape, table[65], jnp.int32) != 0
        whole[2 * side + slot] = own + jnp.where(pick, near, far)
        whole[2 * (1 - side) + slot] = last + jnp.where(pick, far, near)

    def load(position):
        start = pl.multiple_of(((position & 15) >> 1) * 128, 128)
        return whole[position >> 4, :, pl.ds(start, 128)]

    def dest(k, carry):
        for half in range(2):
            tile = 2 * k + half
            value = half_tiles(load, table[2 * tile], table[2 * tile + 1])
            own = grad[:, pl.ds(pl.multiple_of(tile * 128, 128), 128)].astype(jnp.float32)
            out[k, :, half * 128:(half + 1) * 128] = (own + value).astype(jnp.bfloat16)
        return carry

    lax.fori_loop(0, 16, dest, 0)


def combine(table, grad, parts):
    vmem = pl.BlockSpec(memory_space=pltpu.VMEM)
    return pl.pallas_call(
        combine_kernel,
        out_shape=jax.ShapeDtypeStruct((16, ROWS, 256), jnp.bfloat16),
        in_specs=[pl.BlockSpec(memory_space=pltpu.SMEM)] + [vmem] * 5,
        out_specs=vmem,
        scratch_shapes=[pltpu.VMEM((4, ROWS, 1024), jnp.float32)],
        compiler_params=pltpu.CompilerParams(vmem_limit_bytes=24 * MIB),
        cost_estimate=pl.CostEstimate(flops=10**6, bytes_accessed=2 * MIB, transcendentals=0),
        name="combine",
    )(table, grad, *parts)


def attend_kernel(query, key, value, grad, seg_col, seg_row, dquery, dkey, dvalue, kacc, vacc):
    scale = 1.0 / math.sqrt(HD)
    step = 256
    across = (((1,), (1,)), ((), ()))
    down = (((0,), (0,)), ((), ()))
    all_grad = grad[...].reshape(LEN, HD)
    kacc[...] = jnp.zeros_like(kacc)
    vacc[...] = jnp.zeros_like(vacc)
    for i in range(LEN // step):
        low, high = i * step, (i + 1) * step
        start = max(0, low - 512)
        width = high - start
        q = query[0, low:high]
        g = all_grad[low:high]
        k = key[0, start:high]
        v = value[0, start:high]
        scores = lax.dot_general(q, k, across, preferred_element_type=jnp.float32)
        same = seg_col[0, low:high] == seg_row[0, :, start:high]
        place_q = (low - start) + lax.broadcasted_iota(jnp.int32, (step, width), 0)
        place_k = lax.broadcasted_iota(jnp.int32, (step, width), 1)
        scores = jnp.where((place_k <= place_q) & same, scores, masked_fill)
        peak = jnp.max(scores, axis=1, keepdims=True)
        exponent = jnp.exp2((scores - peak) * (scale * math.log2(math.e)))
        prob = exponent * (1.0 / jnp.sum(exponent, axis=1, keepdims=True))
        pgrad = lax.dot_general(g, v, across, preferred_element_type=jnp.float32)
        delta = jnp.sum(prob * pgrad, axis=1, keepdims=True)
        sgrad = (prob * (pgrad - delta)).astype(jnp.bfloat16)
        half = prob.astype(jnp.bfloat16)
        dquery[0, low:high] = (scale * jnp.dot(sgrad, k, preferred_element_type=jnp.float32)).astype(jnp.bfloat16)
        kacc[start:high] += lax.dot_general(sgrad, q, down, preferred_element_type=jnp.float32)
        vacc[start:high] += lax.dot_general(half, g, down, preferred_element_type=jnp.float32)
    dkey[0] = (scale * kacc[...]).astype(jnp.bfloat16)
    dvalue[0] = vacc[...].astype(jnp.bfloat16)


def attend(queries, keys, values, grads, segments):
    flat = pl.BlockSpec((1, LEN, HD), lambda b, h: (b, 0, h))
    return pl.pallas_call(
        attend_kernel,
        grid=(2, 2),
        out_shape=[jax.ShapeDtypeStruct((2, LEN, 256), jnp.bfloat16)] * 3,
        in_specs=[
            flat,
            flat,
            flat,
            pl.BlockSpec((16, 1, 64, HD), lambda b, h: (0, b, 0, h)),
            pl.BlockSpec((1, LEN, 1), lambda b, h: (b, 0, 0)),
            pl.BlockSpec((1, 1, LEN), lambda b, h: (b, 0, 0)),
        ],
        out_specs=[flat, flat, flat],
        scratch_shapes=[pltpu.VMEM((LEN, HD), jnp.float32)] * 2,
        compiler_params=pltpu.CompilerParams(vmem_limit_bytes=48 * MIB),
        cost_estimate=pl.CostEstimate(flops=5 * 10**9, bytes_accessed=8 * MIB, transcendentals=4 * 10**6),
        name="attend",
    )(queries, keys, values, grads, segments.reshape(2, LEN, 1), segments.reshape(2, 1, LEN))


def per_device(
    queries, keys, values, ffn_hidden, out_grad, butterfly, segments, up_weight, down_weight
):
    bits = Bits(butterfly)
    tensor = lax.axis_index("tensor")
    seq = lax.axis_index("seq")
    zpos = tensor & 3
    qpos = ((seq >> 2) << 1) | (seq & 1)
    high_z = (bits.kind == 1).astype(jnp.int32)
    side = (zpos >> high_z) & 1

    ranks = bits.rank(butterfly)
    match = ranks[:, None, :] == jnp.arange(NNZ, dtype=jnp.int32)[None, :, None]
    order = jnp.sum(jnp.where(match, jnp.arange(NNZ, dtype=jnp.int32)[None, None, :], 0), axis=2, dtype=jnp.int32)
    packed = pack_weights(down_weight, up_weight, order, 2 * qpos)

    packed, hidden = lax.switch(
        jnp.maximum(bits.kind - 1, 0), [functools.partial(align, kind) for kind in range(1, 5)], packed, ffn_hidden
    )

    place = jnp.arange(NBLK, dtype=jnp.int32)
    source = bits.block((place >> 4) ^ (2 * side), place & 15)
    from_y = [packed] + [flip(packed, "tensor", 4 * d) for d in (1, 2, 3)]
    own_side, other_side = gather_columns(out_grad.reshape(ROWS, D), source, 2, 2)
    chunks = [
        jnp.where(high_z == 1, own_side, other_side),
        jnp.where(high_z == 1, other_side, own_side),
        other_side,
    ]
    ypos = tensor >> 2
    shares = [lax.dynamic_slice_in_dim(hidden, 8 * (ypos ^ d), 8, 0) for d in range(4)]
    gathered = jnp.stack(from_y)
    tied = tie(gathered, *chunks)
    gathered, chunks = tied[0], tied[1:4]
    hidden = [shares[0]] + [flip(shares[d], "tensor", 4 * d) for d in (1, 2, 3)]
    grads = [flip(chunks[d - 1], "tensor", d) for d in (1, 2, 3)]

    right = flip(gathered, "seq", 4)
    left = flip(gathered, "seq", 12)
    right, left, hidden[1], hidden[3], grads[1] = tie(right, left, hidden[1], hidden[3], grads[1])
    across_a = flip(left[:2], "seq", 4)
    across_b = flip(right[2:], "seq", 12)
    across_a, across_b, hidden[2], grads[0], grads[2] = tie(across_a, across_b, hidden[2], grads[0], grads[2])
    mine = [gathered, right, left, across_a, across_b]
    weights = mine + [flip(part, "seq", 1) for part in mine]
    slopes = [
        gelu_slope(part.astype(jnp.float32)).astype(jnp.bfloat16).reshape(8 * 64, 4 * FB) for part in hidden
    ]

    own_blocks = lax.dynamic_index_in_dim(
        jnp.stack([blocks_of(tensor, kind) for kind in range(5)]), bits.kind, 0, keepdims=False
    )
    own_slots = bits.coset(own_blocks) & 1
    present = jnp.any(own_slots[:, :, None] == jnp.arange(2, dtype=jnp.int32), axis=1).astype(jnp.int32)
    table = jnp.concatenate([jnp.stack([zpos, qpos]).astype(jnp.int32), present.reshape(-1)])
    lanes = jnp.broadcast_to(own_slots[:, None, :, None], (4, 1, 4, FB)).reshape(4, 1, 4 * FB)
    parts = ffn(table, lanes, weights, slopes, [own_side] + grads, 2)

    places = bits.coset(place) * NNZ + bits.rank(place)
    table = jnp.concatenate([places, jnp.stack([side, high_z]).astype(jnp.int32)])
    parts = [parts[0]] + [flip(parts[d], "tensor", d) for d in (1, 2, 3)]
    heads = combine(table, out_grad.reshape(ROWS, D), parts)
    arrived = lax.all_to_all(heads, "seq", split_axis=0, concat_axis=0, tiled=True)
    return tuple(attend(queries, keys, values, arrived.reshape(16, 2, 64, 256), segments))


def solution(mesh):
    placed = (
        P("tensor", None, "seq"),
        P("tensor", None, "seq"),
        P("tensor", None, "seq"),
        P(None, "seq", "tensor"),
        P("tensor", "seq", None),
        P("tensor", None),
        P("tensor", None),
        P("tensor", None, None, None),
        P("tensor", None, None, None),
    )
    return jax.shard_map(
        per_device,
        mesh=mesh,
        in_specs=placed,
        out_specs=(P("tensor", None, "seq"), P("tensor", None, "seq"), P("tensor", None, "seq")),
        check_vma=False,
    )
```

```python
import functools
import math

import jax
import jax.numpy as jnp
from jax import lax
from jax.experimental import pallas as pl
from jax.experimental.pallas import tpu as pltpu
from jax.sharding import PartitionSpec as P

D = 4096
HD = 128
FF = 11264
NBLK = 64
NNZ = 16
DB = 64
FB = 176
LEN = 1024
ROWS = 128
MIB = 1 << 20

masked_fill = -1e30


def gelu_slope(hidden):
    cumulative = 0.5 * (1.0 + jax.scipy.special.erf(hidden * 0.7071067811865476))
    return cumulative + hidden * jnp.exp(-0.5 * hidden * hidden) * 0.3989422804014327


def flip(array, axis, mask):
    return lax.ppermute(array, axis, [(i, i ^ mask) for i in range(16)])


def swapped_index(tensor, kind):
    if kind not in (2, 3):
        return tensor
    low, high = tensor & 1, (tensor >> kind) & 1
    return (tensor & ~((1 << kind) | 1)) | (low << kind) | high


def blocks_of(tensor, kind):
    local = jnp.arange(4, dtype=jnp.int32)
    holders = jnp.stack([swapped_index(tensor ^ (4 * piece), kind) for piece in range(4)]).astype(jnp.int32)[:, None]
    if kind == 4:
        return (holders ^ (local >> 1)[None, :]) * 4 + 2 * (tensor & 1) + (local & 1)[None, :]
    return holders * 4 + local[None, :]


def align(kind, array, axis):
    if kind < 2:
        return array
    if kind < 4:
        return lax.ppermute(array, "tensor", [(i, swapped_index(i, kind)) for i in range(16)])
    low = lax.axis_index("tensor") & 1
    half = array.shape[axis] // 2
    own = lax.dynamic_slice_in_dim(array, half * low, half, axis)
    other = flip(lax.dynamic_slice_in_dim(array, half * (1 - low), half, axis), "tensor", 1)
    return jnp.concatenate([own, other], axis=axis)


def align_all(kind, packed, hidden):
    packed, hidden = align(kind, packed, 1), align(kind, hidden, 2)
    ypos = lax.axis_index("tensor") >> 2
    return (packed,) + tuple(lax.dynamic_slice_in_dim(hidden, 8 * (ypos ^ d), 8, 0) for d in range(4))


def tie(*arrays):
    return lax.optimization_barrier(arrays)


class Bits:
    def __init__(self, butterfly):
        row = butterfly[0]
        span = lax.reduce(row ^ row[0], jnp.int32(0), lax.bitwise_or, (0,))
        missing = 63 & ~span
        zpart = missing & 12
        swapped = jnp.where((missing & 16) != 0, 16, jnp.where((missing & 32) != 0, 32, 2))
        by_swap = jnp.where(swapped == 16, 2, jnp.where(swapped == 32, 3, 4))
        by_z = jnp.where(zpart == 8, 8, 4)
        self.missing = missing
        self.high = jnp.where(zpart == 0, swapped, by_z)
        self.low = missing ^ self.high
        self.kind = jnp.where(zpart == 0, by_swap, by_z >> 3)

    def coset(self, block):
        return 2 * ((block & self.high) != 0).astype(jnp.int32) + ((block & self.low) != 0).astype(jnp.int32)

    def rank(self, block):
        total = jnp.zeros_like(block)
        below = jnp.int32(0)
        for i in range(6):
            kept = 1 - ((self.missing >> i) & 1)
            total = total + ((((block >> i) & 1) * kept) << below)
            below = below + kept
        return total

    def block(self, coset, rank):
        total = jnp.zeros_like(rank)
        below = jnp.int32(0)
        for i in range(6):
            gone = (self.missing >> i) & 1
            of_coset = jnp.where(self.high == (1 << i), coset >> 1, coset & 1)
            bit = jnp.where(gone == 1, of_coset, (rank >> below) & 1)
            total = total | (bit << i)
            below = below + 1 - gone
        return total


def half_tiles(load, first, second):
    left = pltpu.roll(load(first), 64 * (first & 1), 1)
    right = pltpu.roll(load(second), 64 * (1 - (second & 1)), 1)
    lane = lax.broadcasted_iota(jnp.int32, left.shape, 1)
    return jnp.where(lane < 64, left, right)


def gather_columns_kernel(count, table, grad, *outs):
    def load(block):
        start = pl.multiple_of((block >> 1) * 128, 128)
        return grad[:, pl.ds(start, 128)].astype(jnp.float32)

    for target, out in enumerate(outs):
        for slot in range(count):

            def tile(i, carry, target=target, out=out, slot=slot):
                at = (target * count + slot) * 16 + 2 * i
                value = half_tiles(load, table[at], table[at + 1])
                out[slot, :, pl.ds(pl.multiple_of(i * 128, 128), 128)] = value.astype(jnp.bfloat16)
                return carry

            lax.fori_loop(0, 8, tile, 0)


def gather_columns(grad, table, targets, count):
    smem = pl.BlockSpec(memory_space=pltpu.SMEM)
    vmem = pl.BlockSpec(memory_space=pltpu.VMEM)
    return pl.pallas_call(
        functools.partial(gather_columns_kernel, count),
        out_shape=[jax.ShapeDtypeStruct((count, ROWS, 1024), jnp.bfloat16)] * targets,
        in_specs=[smem, vmem],
        out_specs=[vmem] * targets,
        compiler_params=pltpu.CompilerParams(vmem_limit_bytes=24 * MIB),
        name="gather_columns",
    )(table, grad)


def pack_weights_kernel(order, *refs):
    out = refs[16]
    eye = (
        lax.broadcasted_iota(jnp.int32, (2 * DB, 2 * DB), 0) == lax.broadcasted_iota(jnp.int32, (2 * DB, 2 * DB), 1)
    ).astype(jnp.bfloat16)
    for kind in range(2):
        for local in range(4):
            pair = [refs[(kind * 4 + local) * 2 + rank][0, 0] for rank in range(2)]
            both = jnp.concatenate(pair, axis=0)
            turned = lax.dot_general(both, eye, (((0,), (0,)), ((), ())), preferred_element_type=jnp.float32)
            out[kind, local * FB:(local + 1) * FB] = turned.astype(jnp.bfloat16)


def pack_weights(down, up, order, first):
    def spec(local, rank):
        return pl.BlockSpec((1, 1, DB, FB), lambda i, order: (local, order[local * 2 + rank], 0, 0))

    grid = pltpu.PrefetchScalarGridSpec(
        num_scalar_prefetch=1,
        grid=(1,),
        in_specs=[spec(local, rank) for local in range(4) for rank in range(2)] * 2,
        out_specs=pl.BlockSpec((2, 4 * FB, 2 * DB), lambda i, order: (0, 0, 0)),
    )
    chosen = lax.dynamic_slice_in_dim(order, first, 2, 1).reshape(8)
    return pl.pallas_call(
        pack_weights_kernel,
        grid_spec=grid,
        out_shape=jax.ShapeDtypeStruct((2, 4 * FB, 2 * DB), jnp.bfloat16),
        name="pack_weights",
    )(chosen, *[down] * 8, *[up] * 8)


WEIGHT_PARTS = ((0, 0, 4), (2, 0, 4), (6, 0, 4), (4, 0, 2), (4, 2, 4), (1, 0, 4), (3, 0, 4), (7, 0, 4), (5, 0, 2), (5, 2, 4))


def ffn_kernel(table, *refs):
    weights, slopes, grads = refs[:10], refs[10:14], refs[14:18]
    outs = refs[18:22]
    wbuf, sbuf, gbuf, acc, wsem, ssem, gsem = refs[22:]
    zpos, qpos = table[0], table[1]
    early, weight_copies = [], [[], [], [], []]
    for z in range(4):
        early.append(pltpu.make_async_copy(grads[z], gbuf.at[:, z], gsem.at[z]))
        for y in range(4):
            source = slopes[y].at[pl.ds(pl.multiple_of((zpos ^ z) * ROWS, ROWS), ROWS)]
            early.append(pltpu.make_async_copy(source, sbuf.at[y, z], ssem.at[y * 4 + z]))
    for i, (mask, first, last) in enumerate(WEIGHT_PARTS):
        columns = pl.ds(pl.multiple_of((qpos ^ mask) * 2 * DB, 2 * DB), 2 * DB)
        for y in range(first, last):
            weight_copies[y].append(
                pltpu.make_async_copy(weights[i].at[y - first], wbuf.at[y, :, :, columns], wsem.at[i * 4 + y])
            )
    for copy in early + weight_copies[0] + weight_copies[1] + weight_copies[2] + weight_copies[3]:
        copy.start()
    acc[...] = jnp.zeros_like(acc)
    for copy in early:
        copy.wait()

    for y in range(4):
        for copy in weight_copies[y]:
            copy.wait()

        first, second = table[2 + 2 * y], table[3 + 2 * y]

        @pl.when(first + second == 1)
        def _(y=y, second=second):
            grad = gbuf[second].reshape(4 * ROWS, 1024)
            hidden = lax.dot_general(grad, wbuf[y, 0], (((1,), (1,)), ((), ())), preferred_element_type=jnp.float32)
            slope = sbuf[y].reshape(4 * ROWS, 4 * FB).astype(jnp.float32)
            acc[second] += jnp.dot(
                (hidden * slope).astype(jnp.bfloat16), wbuf[y, 1], preferred_element_type=jnp.float32
            )

        @pl.when(first + second == 2)
        def _(y=y):
            for local in range(4):
                slot = table[10 + 4 * y + local]
                rows = slice(local * FB, (local + 1) * FB)
                grad = gbuf[slot].reshape(4 * ROWS, 1024)
                hidden = lax.dot_general(
                    grad, wbuf[y, 0, rows], (((1,), (1,)), ((), ())), preferred_element_type=jnp.float32
                )
                slope = sbuf[y, :, :, rows].reshape(4 * ROWS, FB).astype(jnp.float32)
                acc[slot] += jnp.dot(
                    (hidden * slope).astype(jnp.bfloat16), wbuf[y, 1, rows], preferred_element_type=jnp.float32
                )

    for z in range(4):
        outs[z][...] = acc[:, z * ROWS:(z + 1) * ROWS].astype(jnp.bfloat16)


def ffn(table, weights, slopes, grads):
    count = 2
    hbm = pl.BlockSpec(memory_space=pl.ANY)
    vmem = pl.BlockSpec(memory_space=pltpu.VMEM)
    return pl.pallas_call(
        ffn_kernel,
        out_shape=[jax.ShapeDtypeStruct((count, ROWS, 1024), jnp.bfloat16)] * 4,
        in_specs=[pl.BlockSpec(memory_space=pltpu.SMEM)] + [hbm] * 18,
        out_specs=[vmem] * 4,
        scratch_shapes=[
            pltpu.VMEM((4, 2, 4 * FB, 16 * DB), jnp.bfloat16),
            pltpu.VMEM((4, 4, ROWS, 4 * FB), jnp.bfloat16),
            pltpu.VMEM((count, 4, ROWS, 1024), jnp.bfloat16),
            pltpu.VMEM((count, 4 * ROWS, 1024), jnp.float32),
            pltpu.SemaphoreType.DMA((40,)),
            pltpu.SemaphoreType.DMA((16,)),
            pltpu.SemaphoreType.DMA((4,)),
        ],
        compiler_params=pltpu.CompilerParams(vmem_limit_bytes=52 * MIB),
        cost_estimate=pl.CostEstimate(flops=6 * 10**9, bytes_accessed=24 * MIB, transcendentals=0),
        name="ffn",
    )(table, *weights, *slopes, *grads)


def combine_kernel(table, grad, p0, p1, p2, p3, out, whole):
    side = table[64]
    for slot in range(2):
        own, near, far, last = [part[slot].astype(jnp.float32) for part in (p0, p1, p2, p3)]
        pick = jnp.full(near.shape, table[65], jnp.int32) != 0
        whole[2 * side + slot] = own + jnp.where(pick, near, far)
        whole[2 * (1 - side) + slot] = last + jnp.where(pick, far, near)

    def load(position):
        start = pl.multiple_of(((position & 15) >> 1) * 128, 128)
        return whole[position >> 4, :, pl.ds(start, 128)]

    def dest(k, carry):
        for half in range(2):
            tile = 2 * k + half
            value = half_tiles(load, table[2 * tile], table[2 * tile + 1])
            own = grad[:, pl.ds(pl.multiple_of(tile * 128, 128), 128)].astype(jnp.float32)
            out[k, :, half * 128:(half + 1) * 128] = (own + value).astype(jnp.bfloat16)
        return carry

    lax.fori_loop(0, 16, dest, 0)


def combine(table, grad, parts):
    vmem = pl.BlockSpec(memory_space=pltpu.VMEM)
    return pl.pallas_call(
        combine_kernel,
        out_shape=jax.ShapeDtypeStruct((16, ROWS, 256), jnp.bfloat16),
        in_specs=[pl.BlockSpec(memory_space=pltpu.SMEM)] + [vmem] * 5,
        out_specs=vmem,
        scratch_shapes=[pltpu.VMEM((4, ROWS, 1024), jnp.float32)],
        compiler_params=pltpu.CompilerParams(vmem_limit_bytes=24 * MIB),
        cost_estimate=pl.CostEstimate(flops=10**6, bytes_accessed=2 * MIB, transcendentals=0),
        name="combine",
    )(table, grad, *parts)


def attend_kernel(query, key, value, grad, seg_col, seg_row, dquery, dkey, dvalue, kacc, vacc):
    scale = 1.0 / math.sqrt(HD)
    step = 256
    across = (((1,), (1,)), ((), ()))
    down = (((0,), (0,)), ((), ()))
    all_grad = grad[...].reshape(LEN, HD)
    kacc[...] = jnp.zeros_like(kacc)
    vacc[...] = jnp.zeros_like(vacc)
    for i in range(LEN // step):
        low, high = i * step, (i + 1) * step
        start = max(0, low - 512)
        width = high - start
        q = query[0, low:high]
        g = all_grad[low:high]
        k = key[0, start:high]
        v = value[0, start:high]
        scores = lax.dot_general(q, k, across, preferred_element_type=jnp.float32)
        same = seg_col[0, low:high] == seg_row[0, :, start:high]
        place_q = (low - start) + lax.broadcasted_iota(jnp.int32, (step, width), 0)
        place_k = lax.broadcasted_iota(jnp.int32, (step, width), 1)
        scores = jnp.where((place_k <= place_q) & same, scores, masked_fill)
        peak = jnp.max(scores, axis=1, keepdims=True)
        exponent = jnp.exp2((scores - peak) * (scale * math.log2(math.e)))
        prob = exponent * (1.0 / jnp.sum(exponent, axis=1, keepdims=True))
        pgrad = lax.dot_general(g, v, across, preferred_element_type=jnp.float32)
        delta = jnp.sum(prob * pgrad, axis=1, keepdims=True)
        sgrad = (prob * (pgrad - delta)).astype(jnp.bfloat16)
        half = prob.astype(jnp.bfloat16)
        dquery[0, low:high] = (scale * jnp.dot(sgrad, k, preferred_element_type=jnp.float32)).astype(jnp.bfloat16)
        kacc[start:high] += lax.dot_general(sgrad, q, down, preferred_element_type=jnp.float32)
        vacc[start:high] += lax.dot_general(half, g, down, preferred_element_type=jnp.float32)
    dkey[0] = (scale * kacc[...]).astype(jnp.bfloat16)
    dvalue[0] = vacc[...].astype(jnp.bfloat16)


def attend(queries, keys, values, grads, segments):
    flat = pl.BlockSpec((1, LEN, HD), lambda b, h: (b, 0, h))
    return pl.pallas_call(
        attend_kernel,
        grid=(2, 2),
        out_shape=[jax.ShapeDtypeStruct((2, LEN, 256), jnp.bfloat16)] * 3,
        in_specs=[
            flat,
            flat,
            flat,
            pl.BlockSpec((16, 1, 64, HD), lambda b, h: (0, b, 0, h)),
            pl.BlockSpec((1, LEN, 1), lambda b, h: (b, 0, 0)),
            pl.BlockSpec((1, 1, LEN), lambda b, h: (b, 0, 0)),
        ],
        out_specs=[flat, flat, flat],
        scratch_shapes=[pltpu.VMEM((LEN, HD), jnp.float32)] * 2,
        compiler_params=pltpu.CompilerParams(vmem_limit_bytes=48 * MIB),
        cost_estimate=pl.CostEstimate(flops=5 * 10**9, bytes_accessed=8 * MIB, transcendentals=4 * 10**6),
        name="attend",
    )(queries, keys, values, grads, segments.reshape(2, LEN, 1), segments.reshape(2, 1, LEN))


def per_device(
    queries, keys, values, ffn_hidden, out_grad, butterfly, segments, up_weight, down_weight
):
    bits = Bits(butterfly)
    tensor = lax.axis_index("tensor")
    seq = lax.axis_index("seq")
    zpos = tensor & 3
    qpos = ((seq >> 2) << 1) | (seq & 1)
    high_z = (bits.kind == 1).astype(jnp.int32)
    side = (zpos >> high_z) & 1

    ranks = bits.rank(butterfly)
    match = ranks[:, None, :] == jnp.arange(NNZ, dtype=jnp.int32)[None, :, None]
    order = jnp.sum(jnp.where(match, jnp.arange(NNZ, dtype=jnp.int32)[None, None, :], 0), axis=2, dtype=jnp.int32)
    packed = pack_weights(down_weight, up_weight, order, 2 * qpos)

    branch = jnp.maximum(bits.kind - 1, 0)
    packed, *shares = lax.switch(
        branch, [functools.partial(align_all, kind) for kind in range(1, 5)], packed, ffn_hidden
    )

    place = jnp.arange(NBLK, dtype=jnp.int32)
    source = bits.block((place >> 4) ^ (2 * side), place & 15)
    from_y = [packed] + [flip(packed, "tensor", 4 * d) for d in (1, 2, 3)]
    own_side, other_side = gather_columns(out_grad.reshape(ROWS, D), source, 2, 2)
    chunks = [
        jnp.where(high_z == 1, own_side, other_side),
        jnp.where(high_z == 1, other_side, own_side),
        other_side,
    ]
    gathered = jnp.stack(from_y)
    tied = tie(gathered, *chunks)
    gathered, chunks = tied[0], tied[1:4]
    hidden = [shares[0]] + [flip(shares[d], "tensor", 4 * d) for d in (1, 2, 3)]
    grads = [flip(chunks[d - 1], "tensor", d) for d in (1, 2, 3)]

    right = flip(gathered, "seq", 4)
    left = flip(gathered, "seq", 12)
    right, left, hidden[1], hidden[3], grads[1] = tie(right, left, hidden[1], hidden[3], grads[1])
    across_a = flip(left[:2], "seq", 4)
    across_b = flip(right[2:], "seq", 12)
    across_a, across_b, hidden[2], grads[0], grads[2] = tie(across_a, across_b, hidden[2], grads[0], grads[2])
    mine = [gathered, right, left, across_a, across_b]
    weights = mine + [flip(part, "seq", 1) for part in mine]
    slopes = [
        gelu_slope(part.astype(jnp.float32)).astype(jnp.bfloat16).reshape(8 * 64, 4 * FB) for part in hidden
    ]

    own_blocks = lax.dynamic_index_in_dim(
        jnp.stack([blocks_of(tensor, kind) for kind in range(5)]), bits.kind, 0, keepdims=False
    )
    own_slots = bits.coset(own_blocks) & 1
    present = jnp.any(own_slots[:, :, None] == jnp.arange(2, dtype=jnp.int32), axis=1).astype(jnp.int32)
    table = jnp.concatenate([jnp.stack([zpos, qpos]).astype(jnp.int32), present.reshape(-1), own_slots.reshape(-1)])
    parts = ffn(table, weights, slopes, [own_side] + grads)

    places = bits.coset(place) * NNZ + bits.rank(place)
    table = jnp.concatenate([places, jnp.stack([side, high_z]).astype(jnp.int32)])
    parts = [parts[0]] + [flip(parts[d], "tensor", d) for d in (1, 2, 3)]
    heads = combine(table, out_grad.reshape(ROWS, D), parts)
    arrived = lax.all_to_all(heads, "seq", split_axis=0, concat_axis=0, tiled=True)
    return tuple(attend(queries, keys, values, arrived.reshape(16, 2, 64, 256), segments))


def solution(mesh):
    placed = (
        P("tensor", None, "seq"),
        P("tensor", None, "seq"),
        P("tensor", None, "seq"),
        P(None, "seq", "tensor"),
        P("tensor", "seq", None),
        P("tensor", None),
        P("tensor", None),
        P("tensor", None, None, None),
        P("tensor", None, None, None),
    )
    return jax.shard_map(
        per_device,
        mesh=mesh,
        in_specs=placed,
        out_specs=(P("tensor", None, "seq"), P("tensor", None, "seq"), P("tensor", None, "seq")),
        check_vma=False,
    )
```
